256 devices in a mesh: ctx: 32 (over z, x_lo, core), head: 8 (over x_hi, y).
Axes of the slice: x: 4 (x_hi: 2, x_lo: 2; x = x_hi * 2 + x_lo), y: 4, z: 8, core: 2. Of those that a mesh axis runs over, the one named last changes fastest.
Arguments:
- queries: bfloat16 [4096, 8192], P('ctx', 'head'), parts along dimension 1, may hold values from -6 to 6
- keys: bfloat16 [4096, 1024], P('ctx', 'head'), parts along dimension 1, may hold values from -6 to 6
- values: bfloat16 [4096, 1024], P('ctx', 'head'), parts along dimension 1, may hold values from -6 to 6
- out_grad: bfloat16 [4096, 8192], P('ctx', 'head'), parts along dimension 1, may hold values from -3 to 3
Outputs:
- attention: bfloat16 [4096, 8192], P('ctx', 'head'), parts along dimension 1
- query_grad: bfloat16 [4096, 8192], P('ctx', 'head'), parts along dimension 1
- key_grad: bfloat16 [4096, 1024], P('ctx', 'head'), parts along dimension 1
- value_grad: bfloat16 [4096, 1024], P('ctx', 'head'), parts along dimension 1
The draws below stay inside these ranges and needn't reach their ends.
There are 8 independent parts, one for each index of `head`. The reference program is written for one: setup_inputs(seed, part) draws one part's arguments, and reference() takes and returns one part's arrays. A program takes and returns all parts, laid end to end along the dimension named above; each array names one. Nothing has to cross between parts.
All inputs are finite; a program needn't handle non-finite values.
Results may differ from the reference program's by a relative error of at most 0.035.
Values may be sent and summed in bfloat16 or wider, within the bound.
A program may use at most 64 MiB of HBM per device.

```python
import jax
import jax.numpy as jnp
from jax import lax

HQ = 8
HD = 128
TOK_DEV = 128
TOKENS = 4096


def draw_queries(key, part):
    key = jax.random.fold_in(key, 11)
    first_key = jax.random.fold_in(key, 0)
    base = jnp.clip(1.5 * jax.random.normal(first_key, (TOKENS * HQ, HD), jnp.float32), -6.0, 6.0)
    return base.reshape(TOKENS, HQ * HD).astype(jnp.bfloat16)


def draw_keys(key, part):
    key = jax.random.fold_in(key, 23)
    base = jnp.clip(1.5 * jax.random.normal(key, (TOKENS, HD), jnp.float32), -6.0, 6.0)
    return base.astype(jnp.bfloat16)


def block_levels(key, extent, cuts, least, top_value):
    gain = 1.0
    for axis_at, shards_of in cuts:
        draws = jax.random.uniform(jax.random.fold_in(jax.random.fold_in(key, 6), axis_at), (shards_of,), jnp.float32, least / len(cuts), top_value / len(cuts))
        gain = gain * jnp.repeat(jnp.exp(draws), extent[axis_at] // shards_of).reshape((-1,) + (1,) * (len(extent) - 1 - axis_at))
    return gain


def bell_draw(key, dims, spread, bound, cuts=(), kind=jnp.bfloat16):
    drawn = spread * jax.random.normal(key, dims, jnp.float32)
    if cuts:
        drawn = drawn * block_levels(key, dims, cuts, -0.22, 0.18)
    return jnp.clip(drawn, -bound, bound).astype(kind)


def setup_inputs(seed: int = 0, part: int = 0) -> dict:
    seeds = jax.random.split(jax.random.key(seed), 5)
    own_keys = jax.random.split(jax.random.fold_in(seeds[4], part), 5)
    queries = draw_queries(jax.random.fold_in(jax.random.fold_in(seeds[4], part), 71), part)
    keys = draw_keys(jax.random.fold_in(jax.random.fold_in(seeds[4], part), 71), part)
    values = bell_draw(own_keys[2], (TOKENS, HD), 1.0, 6.0, ((0, 32),))
    out_grad = bell_draw(own_keys[3], (TOKENS, HQ * HD), 0.5, 3.0, ((0, 32),))
    return {"queries": queries, "keys": keys, "values": values, "out_grad": out_grad}


def reference(queries, keys, values, out_grad):
    length = keys.shape[0]
    head_size = keys.shape[1]
    per_token = queries.shape[1] // head_size
    block_tokens = TOK_DEV // 2
    block_count = length // block_tokens
    score_scale = HD ** -0.5
    query_blocks = queries.reshape(block_count, block_tokens * per_token, head_size)
    grad_blocks = out_grad.reshape(block_count, block_tokens * per_token, head_size)
    key_pos = jnp.arange(length, dtype=jnp.int32)[None, :]
    row_token = (jnp.arange(block_tokens * per_token, dtype=jnp.int32) // per_token)[:, None]

    def one_block(carried, block_item):
        key_acc, value_acc = carried
        query_rows, grad_rows, block_index = block_item
        visible = key_pos <= block_index * block_tokens + row_token
        scores = jnp.dot(query_rows, keys.T, preferred_element_type=jnp.float32) * score_scale
        scores = jnp.where(visible, scores, -1e30)
        row_top = jnp.max(scores, axis=1, keepdims=True)
        row_total = jnp.sum(jnp.where(visible, jnp.exp(scores - row_top), 0.0), axis=1, keepdims=True)
        row_lse = row_top + jnp.log(row_total)
        probabilities = jnp.where(visible, jnp.exp(scores - row_lse), 0.0)
        weights = probabilities.astype(jnp.bfloat16)
        attended = jnp.dot(weights, values, preferred_element_type=jnp.float32).astype(jnp.bfloat16)
        attended = lax.optimization_barrier(attended)
        row_delta = jnp.sum(grad_rows.astype(jnp.float32) * attended.astype(jnp.float32), axis=1, keepdims=True)
        dprobs = jnp.dot(grad_rows, values.T, preferred_element_type=jnp.float32)
        dscores = (probabilities * (dprobs - row_delta) * score_scale).astype(jnp.bfloat16)
        query_part = jnp.dot(dscores, keys, preferred_element_type=jnp.float32).astype(jnp.bfloat16)
        key_acc = key_acc + jnp.dot(dscores.T, query_rows, preferred_element_type=jnp.float32)
        value_acc = value_acc + jnp.dot(weights.T, grad_rows, preferred_element_type=jnp.float32)
        return (key_acc, value_acc), (attended, query_part)

    start_acc = (jnp.zeros((length, head_size), jnp.float32), jnp.zeros((length, head_size), jnp.float32))
    block_ids = jnp.arange(block_count, dtype=jnp.int32)
    (key_acc, value_acc), (attended, query_part) = lax.scan(one_block, start_acc, (query_blocks, grad_blocks, block_ids))
    attention = attended.reshape(length, per_token * head_size)
    query_grad = query_part.reshape(length, per_token * head_size)
    return (attention, query_grad, key_acc.astype(jnp.bfloat16), value_acc.astype(jnp.bfloat16))
```

```python
import functools
import math

import jax
import jax.numpy as jnp
from jax import lax
from jax.experimental import pallas as pl
from jax.experimental.pallas import tpu as pltpu
from jax.sharding import PartitionSpec as P

HEADS, HD, TOK, PLANES, QUAD = 8, 128, 128, 8, 4
KEYS, ROWS = QUAD * TOK, HEADS * TOK
SCALE = HD**-0.5
LOG2_SCALE = SCALE * math.log2(math.e)
f32, bf16 = jnp.float32, jnp.bfloat16


def mm(a, b):
    return jnp.dot(a, b, preferred_element_type=f32)


def mm_nt(a, b):
    return lax.dot_general(a, b, (((1,), (1,)), ((), ())), preferred_element_type=f32)


def attend(q, g, k, v, out, dq, grads, qT, gT, E, top, total, block_top, acc, outT, dqT):
    me = lax.axis_index("ctx")
    plane, place = me // QUAD, me % QUAD
    for h in range(HEADS):
        s = slice(h * TOK, (h + 1) * TOK)
        qT[:, s] = q[:, s].T
        gT[:, s] = g[:, s].T

    def forward(b, own):
        rows = pl.ds(pl.multiple_of(b * KEYS, KEYS), KEYS)
        S = mm(k[rows, :], qT[...])
        if own:
            key_at = lax.broadcasted_iota(jnp.int32, (KEYS, ROWS), 0)
            query_at = place * TOK + (lax.broadcasted_iota(jnp.int32, (KEYS, ROWS), 1) & (TOK - 1))
            visible = key_at <= query_at
            S = jnp.where(visible, S, -1e30)
        new_top = jnp.max(S, axis=0, keepdims=True)
        if not own:
            new_top = jnp.maximum(top[...], new_top)
            shrink = jnp.exp2((top[...] - new_top) * LOG2_SCALE)
        e = jnp.exp2((S - new_top) * LOG2_SCALE)
        if own:
            e = jnp.where(visible, e, 0.0)
        eb = e.astype(bf16)
        E[rows, :] = eb
        part = mm(v[rows, :].T, eb)
        if own:
            total[...] = jnp.sum(e, axis=0, keepdims=True)
            acc[...] = part
        else:
            total[...] = total[...] * shrink + jnp.sum(e, axis=0, keepdims=True)
            acc[...] = acc[...] * shrink + part
        top[...] = new_top
        block_top[pl.ds(b, 1), :] = new_top

    forward(plane, True)

    @pl.loop(0, plane)
    def _(b):
        forward(b, False)

    ob = (acc[...] / total[...]).astype(bf16)
    outT[...] = ob
    for h in range(HEADS):
        s = slice(h * TOK, (h + 1) * TOK)
        out[:, s] = ob[:, s].T
    dqT[...] = jnp.zeros_like(dqT)
    grads[...] = jnp.zeros_like(grads)

    @pl.loop(0, plane + 1)
    def _(b):
        rows = pl.ds(pl.multiple_of(b * KEYS, KEYS), KEYS)
        c = jnp.exp2((block_top[pl.ds(b, 1), :] - top[...]) * LOG2_SCALE) / total[...]
        gc = (gT[...].astype(f32) * c).astype(bf16)
        delta = jnp.sum(gc.astype(f32) * outT[...].astype(f32), axis=0, keepdims=True)
        dP = mm(v[rows, :], gc)
        e = E[rows, :]
        dS = (e.astype(f32) * (dP - delta)).astype(bf16)
        dqT[...] += mm(k[rows, :].T, dS)
        dk = mm_nt(qT[...], dS) * SCALE
        dv = mm_nt(gc, e)
        for j in range(QUAD):
            grads[b * QUAD + j, :HD, :] = dk[:, j * TOK : (j + 1) * TOK]
            grads[b * QUAD + j, HD:, :] = dv[:, j * TOK : (j + 1) * TOK]

    for h in range(HEADS):
        s = slice(h * TOK, (h + 1) * TOK)
        dq[:, s] = (dqT[:, s] * SCALE).astype(bf16).T


def local(queries, keys, values, out_grad):
    pair = lax.all_gather(jnp.stack([keys, values]), "ctx", axis=1, tiled=True)
    out, dq, grads = pl.pallas_call(
        attend,
        out_shape=[
            jax.ShapeDtypeStruct((TOK, ROWS), bf16),
            jax.ShapeDtypeStruct((TOK, ROWS), bf16),
            jax.ShapeDtypeStruct((PLANES * QUAD, 2 * HD, TOK), f32),
        ],
        scratch_shapes=[
            pltpu.VMEM((HD, ROWS), bf16),
            pltpu.VMEM((HD, ROWS), bf16),
            pltpu.VMEM((PLANES * KEYS, ROWS), bf16),
            pltpu.VMEM((1, ROWS), f32),
            pltpu.VMEM((1, ROWS), f32),
            pltpu.VMEM((PLANES, ROWS), f32),
            pltpu.VMEM((HD, ROWS), f32),
            pltpu.VMEM((HD, ROWS), bf16),
            pltpu.VMEM((HD, ROWS), f32),
        ],
        compiler_params=pltpu.CompilerParams(vmem_limit_bytes=48 << 20),
    )(queries, out_grad, pair[0], pair[1])
    home = lax.psum_scatter(grads, "ctx", scatter_dimension=0, tiled=True)[0].astype(bf16)
    return out, dq, home[:HD].T, home[HD:].T


def solution(mesh):
    spec = P("ctx", "head")
    return jax.shard_map(local, mesh=mesh, in_specs=(spec,) * 4, out_specs=(spec,) * 4, check_vma=False)
```

```python
import math

import jax
import jax.numpy as jnp
from jax import lax
from jax.experimental import pallas as pl
from jax.experimental.pallas import tpu as pltpu
from jax.sharding import PartitionSpec as P

HEADS, HD, TOK, PLANES, QUAD = 8, 128, 128, 8, 4
KEYS, ROWS = QUAD * TOK, HEADS * TOK
SCALE = HD**-0.5
LOG2_SCALE = SCALE * math.log2(math.e)
X_AHEAD = 4
f32, bf16 = jnp.float32, jnp.bfloat16


def mm(a, b):
    return jnp.dot(a, b, preferred_element_type=f32)


def mm_nt(a, b):
    return lax.dot_general(a, b, (((1,), (1,)), ((), ())), preferred_element_type=f32)


def when(condition):
    return pl.when(condition)


def attend(
    q, g, k, v, out, dq, dk_out, dv_out,
    kv, qT, gT, E, top, total, block_top, acc, outT, dqT,
    G, from_core, H, from_x, Z, from_z,
    z_out, z_in, x_out, x_in, c_out, c_in, gc_out, gc_in, gx_out, gx_in, gz_out, gz_in,
):
    me, head = lax.axis_index("ctx"), lax.axis_index("head")
    plane, place = me // QUAD, me % QUAD
    x, core = place // 2, place % 2
    far = PLANES - 1 - plane

    def at(z, x_, core_):
        return dict(device_id=(z * QUAD + x_ * 2 + core_, head), device_id_type=pl.DeviceIdType.MESH)

    def shard(d, core_, x_):
        return kv.at[d, core_, x_]

    def copy(src, dst, s, r, where):
        return pltpu.make_async_remote_copy(src, dst, s, r, **where)

    def send_z(d):
        return copy(shard(0, core, x), shard(d, core, x), z_out.at[d], z_in.at[d], at(lax.rem(plane + d, PLANES), x, core))

    def send_x(d):
        return copy(shard(d, core, x), shard(d, core, x), x_out.at[d], x_in.at[d], at(plane, 1 - x, core))

    def get_x(d):
        return copy(shard(d, core, 1 - x), shard(d, core, 1 - x), x_out.at[d], x_in.at[d], at(plane, 1 - x, core))

    def send_core(d, j):
        which = x if j == 0 else 1 - x
        return copy(shard(d, core, which), shard(d, core, which), c_out.at[d, j], c_in.at[d, j], at(plane, x, 1 - core))

    def get_core(d, j):
        which = x if j == 0 else 1 - x
        return copy(shard(d, 1 - core, which), shard(d, 1 - core, which), c_out.at[d, j], c_in.at[d, j], at(plane, x, 1 - core))

    def grad_core(d):
        return copy(G.at[d, 1 - core], from_core.at[d], gc_out.at[d], gc_in.at[d], at(plane, x, 1 - core))

    def grad_x(d):
        return copy(H.at[d, 1 - x], from_x.at[d], gx_out.at[d], gx_in.at[d], at(plane, 1 - x, core))

    def grad_z(d):
        return copy(Z.at[d], from_z.at[d], gz_out.at[d], gz_in.at[d], at(lax.rem(plane + PLANES - d, PLANES), x, core))

    barrier = pltpu.get_barrier_semaphore()

    def greet(where):
        pl.semaphore_signal(barrier, inc=1, **where)

    greet(at(plane, x, 1 - core))
    greet(at(plane, 1 - x, core))
    for d in range(1, PLANES):
        greet(at(lax.rem(plane + d, PLANES), x, core))
    kv[0, core, x, :, :HD] = k[...]
    kv[0, core, x, :, HD:] = v[...]
    pl.semaphore_wait(barrier, PLANES + 1)

    send_core(0, 0).start()
    send_x(0).start()
    for z in range(PLANES - 1, 0, -1):

        @when(z > plane)
        def _():
            send_z(z - plane).start()

    for h in range(HEADS):
        s = slice(h * TOK, (h + 1) * TOK)
        qT[:, s] = q[:, s].T
        gT[:, s] = g[:, s].T

    def pass_z(d):
        @when(d <= plane)
        def _():
            send_z(d).wait_recv()
            send_x(d).start()
            send_core(d, 0).start()

    def pass_x(d):
        @when(d <= plane)
        def _():
            get_x(d).wait_recv()
            send_core(d, 1).start()

    def keys_of(d):
        return kv[d, :, :, :, :HD].reshape(KEYS, HD)

    def values_of(d):
        return kv[d, :, :, :, HD:].reshape(KEYS, HD)

    def forward(d, own):
        get_core(d, 0).wait_recv()
        get_core(d, 1).wait_recv()
        S = mm(keys_of(d), qT[...])
        if own:
            row = lax.broadcasted_iota(jnp.int32, (KEYS, ROWS), 0)
            key_at = ((row // TOK) % 2) * (2 * TOK) + (row // (2 * TOK)) * TOK + (row & (TOK - 1))
            query_at = place * TOK + (lax.broadcasted_iota(jnp.int32, (KEYS, ROWS), 1) & (TOK - 1))
            visible = key_at <= query_at
            S = jnp.where(visible, S, -1e30)
        new_top = jnp.max(S, axis=0, keepdims=True)
        if not own:
            new_top = jnp.maximum(top[...], new_top)
            shrink = jnp.exp2((top[...] - new_top) * LOG2_SCALE)
        e = jnp.exp2((S - new_top) * LOG2_SCALE)
        if own:
            e = jnp.where(visible, e, 0.0)
        eb = e.astype(bf16)
        E[d] = eb
        part = mm(values_of(d).T, eb)
        if own:
            total[...] = jnp.sum(e, axis=0, keepdims=True)
            acc[...] = part
        else:
            total[...] = total[...] * shrink + jnp.sum(e, axis=0, keepdims=True)
            acc[...] = acc[...] * shrink + part
        top[...] = new_top
        block_top[pl.ds(d, 1), :] = new_top

    pass_x(0)
    pass_z(1)
    pass_z(2)
    forward(0, True)
    pass_x(1)

    @pl.loop(1, plane + 1)
    def _(d):
        pass_z(d + 2)
        pass_x(d + 1)
        forward(d, False)

    ob = (acc[...] / total[...]).astype(bf16)
    outT[...] = ob
    for h in range(HEADS):
        s = slice(h * TOK, (h + 1) * TOK)
        out[:, s] = ob[:, s].T
    dqT[...] = jnp.zeros_like(dqT)

    def join_core(d):
        grad_core(d).wait_recv()
        for j in range(2):
            H[d, j] = (G[d, core, j].astype(f32) + from_core[d, j].astype(f32)).astype(bf16)
        grad_x(d).start()

    def join_x(d):
        grad_x(d).wait_recv()
        Z[d] = (H[d, x].astype(f32) + from_x[d].astype(f32)).astype(bf16)

    @pl.loop(0, plane + 1)
    def _(step):
        d = plane - step
        c = jnp.exp2((block_top[pl.ds(d, 1), :] - top[...]) * LOG2_SCALE) / total[...]
        gc = (gT[...].astype(f32) * c).astype(bf16)
        delta = jnp.sum(gc.astype(f32) * outT[...].astype(f32), axis=0, keepdims=True)
        dP = mm(values_of(d), gc)
        e = E[d]
        dS = (e.astype(f32) * (dP - delta)).astype(bf16)
        dqT[...] += mm(keys_of(d).T, dS)
        dk = mm_nt(qT[...], dS).astype(bf16)
        dv = mm_nt(gc, e).astype(bf16)
        for j in range(QUAD):
            G[d, j // 2, j % 2, :HD, :] = dk[:, j * TOK : (j + 1) * TOK]
            G[d, j // 2, j % 2, HD:, :] = dv[:, j * TOK : (j + 1) * TOK]
        grad_core(d).start()

        @when(step >= 1)
        def _():
            join_core(d + 1)

        @when(step >= X_AHEAD)
        def _():
            join_x(d + X_AHEAD)
            grad_z(d + X_AHEAD).start()

    join_core(0)
    for d in range(X_AHEAD - 1, 0, -1):

        @when(d <= plane)
        def _():
            join_x(d)
            grad_z(d).start()

    for h in range(HEADS):
        s = slice(h * TOK, (h + 1) * TOK)
        dq[:, s] = (dqT[:, s] * SCALE).astype(bf16).T

    join_x(0)
    dqT[:, : 2 * HD] = Z[0].astype(f32).reshape(2, HD, TOK).transpose(1, 0, 2).reshape(HD, 2 * HD)

    @pl.loop(0, far)
    def _(step):
        d = far - step
        grad_z(d).wait_recv()
        more = from_z[d].astype(f32)
        dqT[:, :HD] += more[:HD]
        dqT[:, HD : 2 * HD] += more[HD:]

    dk_out[...] = (dqT[:, :HD] * SCALE).T.astype(bf16)
    dv_out[...] = dqT[:, HD : 2 * HD].T.astype(bf16)

    @pl.loop(0, plane + 1)
    def _(d):
        send_x(d).wait_send()
        send_core(d, 0).wait_send()
        send_core(d, 1).wait_send()
        grad_core(d).wait_send()
        grad_x(d).wait_send()

        @when(d >= 1)
        def _():
            grad_z(d).wait_send()

    @pl.loop(1, far + 1)
    def _(d):
        send_z(d).wait_send()


def local(queries, keys, values, out_grad):
    dma = pltpu.SemaphoreType.DMA
    return pl.pallas_call(
        attend,
        out_shape=[
            jax.ShapeDtypeStruct((TOK, ROWS), bf16),
            jax.ShapeDtypeStruct((TOK, ROWS), bf16),
            jax.ShapeDtypeStruct((TOK, HD), bf16),
            jax.ShapeDtypeStruct((TOK, HD), bf16),
        ],
        in_specs=[pl.BlockSpec(memory_space=pltpu.VMEM)] * 4,
        out_specs=[pl.BlockSpec(memory_space=pltpu.VMEM)] * 4,
        scratch_shapes=[
            pltpu.VMEM((PLANES, 2, 2, TOK, 2 * HD), bf16),
            pltpu.VMEM((HD, ROWS), bf16),
            pltpu.VMEM((HD, ROWS), bf16),
            pltpu.VMEM((PLANES, KEYS, ROWS), bf16),
            pltpu.VMEM((1, ROWS), f32),
            pltpu.VMEM((1, ROWS), f32),
            pltpu.VMEM((PLANES, ROWS), f32),
            pltpu.VMEM((HD, ROWS), f32),
            pltpu.VMEM((HD, ROWS), bf16),
            pltpu.VMEM((HD, ROWS), f32),
            pltpu.VMEM((PLANES, 2, 2, 2 * HD, TOK), bf16),
            pltpu.VMEM((PLANES, 2, 2 * HD, TOK), bf16),
            pltpu.VMEM((PLANES, 2, 2 * HD, TOK), bf16),
            pltpu.VMEM((PLANES, 2 * HD, TOK), bf16),
            pltpu.VMEM((PLANES, 2 * HD, TOK), bf16),
            pltpu.VMEM((PLANES, 2 * HD, TOK), bf16),
        ]
        + [dma((PLANES,))] * 4
        + [dma((PLANES, 2))] * 2
        + [dma((PLANES,))] * 6,
        compiler_params=pltpu.CompilerParams(
            collective_id=0, has_side_effects=True, vmem_limit_bytes=48 << 20
        ),
    )(queries, out_grad, keys, values)


def solution(mesh):
    spec = P("ctx", "head")
    return jax.shard_map(local, mesh=mesh, in_specs=(spec,) * 4, out_specs=(spec,) * 4, check_vma=False)
```

```python
import math

import jax
import jax.numpy as jnp
from jax import lax
from jax.experimental import pallas as pl
from jax.experimental.pallas import tpu as pltpu
from jax.sharding import PartitionSpec as P

HEADS, HD, TOK, PLANES, QUAD = 8, 128, 128, 8, 4
KEYS, ROWS = QUAD * TOK, HEADS * TOK
SCALE = HD**-0.5
LOG2_SCALE = SCALE * math.log2(math.e)
X_AHEAD = 3
CHUNK = 256
Z_AHEAD = 3
LAST = PLANES - 1
f32, bf16 = jnp.float32, jnp.bfloat16


def mm(a, b):
    return jnp.dot(a, b, preferred_element_type=f32)


def mm_nt(a, b):
    return lax.dot_general(a, b, (((1,), (1,)), ((), ())), preferred_element_type=f32)


def when(condition):
    return pl.when(condition)


def attend(
    q_hbm, g_hbm, k_hbm, v_hbm, out_hbm, dq_hbm, dk_hbm, dv_hbm,
    q, g, k, v, out, dq, dk_out, dv_out, kv, qT, gT, E, top, total, block_top, acc, outT, dqT,
    G, from_core, H, from_x, Z, from_z,
    load, store, z_out, z_in, w_out, w_in, x_out, x_in, c_out, c_in, gc_out, gc_in, gx_out, gx_in, gz_out, gz_in,
):
    me, head = lax.axis_index("ctx"), lax.axis_index("head")
    plane, place = me // QUAD, me % QUAD
    x, core = place // 2, place % 2

    def at(z, x_, core_):
        return dict(device_id=(z * QUAD + x_ * 2 + core_, head), device_id_type=pl.DeviceIdType.MESH)

    def shard(d, core_, x_):
        return kv.at[d, core_, x_]

    def copy(src, dst, s, r, where):
        return pltpu.make_async_remote_copy(src, dst, s, r, **where)

    def send_z(d, src, hops):
        return copy(shard(src, core, x), shard(d, core, x), z_out.at[d], z_in.at[d], at(lax.rem(plane + hops, PLANES), x, core))

    def send_w(d, src, to):
        return copy(shard(src, core, 1 - x), shard(d, core, 1 - x), w_out.at[d], w_in.at[d], at(to, x, core))

    def get_z(d):
        return copy(shard(d, core, x), shard(d, core, x), z_out.at[d], z_in.at[d], at(plane, x, 1 - core))

    def get_w(d):
        return copy(shard(d, core, 1 - x), shard(d, core, 1 - x), w_out.at[d], w_in.at[d], at(plane, x, 1 - core))

    def narrow(d):
        return (d <= 4) | (plane != LAST)

    def direct(d):
        return ((d <= 2) & (plane + d <= LAST)) | ((d >= 5) & (plane + d == LAST))

    def relayed(d):
        return (plane >= 2) & (plane + d - 2 <= LAST)

    def send_own(d):
        return send_z(d, 0, d)

    def relay_up(d):
        return send_z(d, 2, d - 2)

    ROUND = ((6, 7, LAST - 1), (5, 7, LAST - 2), (5, 6, LAST - 1))

    def round_own(i):
        d, src, to = ROUND[i]
        return copy(shard(src, core, x), shard(d, core, x), z_out.at[i], z_in.at[d], at(to, x, core))

    def relay_round(d):
        @when((plane == LAST) & (d == LAST))
        def _():
            round_own(0).start()
            round_own(1).start()

        @when((plane == LAST) & (d == LAST - 1))
        def _():
            round_own(2).start()

    def send_x(d):
        return copy(shard(d, core, x), shard(d, core, x), x_out.at[d], x_in.at[d], at(plane, 1 - x, core))

    def get_x(d):
        return copy(shard(d, core, 1 - x), shard(d, core, 1 - x), x_out.at[d], x_in.at[d], at(plane, 1 - x, core))

    def send_core(d, j):
        which = x if j == 0 else 1 - x
        return copy(shard(d, core, which), shard(d, core, which), c_out.at[d, j], c_in.at[d, j], at(plane, x, 1 - core))

    def get_core(d, j):
        which = x if j == 0 else 1 - x
        return copy(shard(d, 1 - core, which), shard(d, 1 - core, which), c_out.at[d, j], c_in.at[d, j], at(plane, x, 1 - core))

    def grad_core(d):
        return copy(G.at[d, 1 - core], from_core.at[d], gc_out.at[d], gc_in.at[d], at(plane, x, 1 - core))

    def grad_x(d):
        return copy(H.at[d, 1 - x], from_x.at[d], gx_out.at[d], gx_in.at[d], at(plane, 1 - x, core))

    def grad_z(d):
        hops = jnp.where((d == 3) | (d == 4), d - 2, d)
        return copy(Z.at[d], from_z.at[d], gz_out.at[d], gz_in.at[d], at(lax.rem(plane + PLANES - hops, PLANES), x, core))

    wraps = jnp.maximum(plane - 4, 0)

    def block_at(i):
        return jnp.where(i <= 2, i, jnp.where(i < 3 + wraps, plane + 3 - i, i - wraps))

    fetch = [
        pltpu.make_async_copy(src, dst, load.at[i])
        for i, (src, dst) in enumerate(
            ((k_hbm, k), (v_hbm, v), (q_hbm, q), (g_hbm, g))
        )
    ]
    store_out = [
        pltpu.make_async_copy(src, dst, store.at[i])
        for i, (src, dst) in enumerate(
            ((out, out_hbm), (dq, dq_hbm), (dk_out, dk_hbm), (dv_out, dv_hbm))
        )
    ]
    for f in fetch:
        f.start()
    barrier = pltpu.get_barrier_semaphore()

    def greet(where):
        pl.semaphore_signal(barrier, inc=1, **where)

    greet(at(plane, x, 1 - core))
    greet(at(plane, 1 - x, core))
    for d in range(1, PLANES):
        greet(at(lax.rem(plane + d, PLANES), x, core))
    fetch[0].wait()
    fetch[1].wait()
    kv[0, core, x, :, :HD] = k[...]
    kv[0, core, x, :, HD:] = v[...]
    pl.semaphore_wait(barrier, PLANES + 1)

    send_core(0, 0).start()
    send_x(0).start()
    for d in (7, 6, 5, 4, 3, 2, 1):

        @when(direct(d))
        def _():
            send_own(d).start()

    fetch[2].wait()
    fetch[3].wait()
    for h in range(HEADS):
        s = slice(h * TOK, (h + 1) * TOK)
        qT[:, s] = q[:, s].T
        gT[:, s] = g[:, s].T

    def pass_z(i):
        @when(i <= plane)
        def _():
            d = block_at(i)
            get_z(d).wait_recv()
            relay_round(d)

            @when(narrow(d))
            def _():
                send_x(d).start()

            send_core(d, 0).start()

    def relay():
        for d in (4, 3):

            @when(relayed(d))
            def _():
                relay_up(d).start()

    def pass_x(i):
        @when(i <= plane)
        def _():
            d = block_at(i)

            @when(narrow(d))
            def _():
                get_x(d).wait_recv()

            @when(~narrow(d))
            def _():
                get_w(d).wait_recv()

            send_core(d, 1).start()

    def keys_of(d):
        return kv[d, :, :, :, :HD].reshape(KEYS, HD)

    def values_of(d):
        return kv[d, :, :, :, HD:].reshape(KEYS, HD)

    def forward(d, own):
        get_core(d, 0).wait_recv()
        get_core(d, 1).wait_recv()
        cols = [slice(i * CHUNK, (i + 1) * CHUNK) for i in range(ROWS // CHUNK)]
        old = [None if own else (top[:, s], total[:, s], acc[:, s]) for s in cols]
        keys_d, valuesT = keys_of(d), values_of(d).T
        scores = [mm(keys_d, qT[:, s]) for s in cols]
        if own:
            row = lax.broadcasted_iota(jnp.int32, (KEYS, CHUNK), 0)
            key_at = ((row // TOK) % 2) * (2 * TOK) + (row // (2 * TOK)) * TOK + (row & (TOK - 1))
            query_at = place * TOK + (lax.broadcasted_iota(jnp.int32, (KEYS, CHUNK), 1) & (TOK - 1))
            visible = key_at <= query_at
        new = []
        for i, S in enumerate(scores):
            if own:
                S = jnp.where(visible, S, -1e30)
            new_top = jnp.max(S, axis=0, keepdims=True)
            if not own:
                new_top = jnp.maximum(old[i][0], new_top)
            e = jnp.exp2((S - new_top) * LOG2_SCALE)
            if own:
                e = jnp.where(visible, e, 0.0)
            eb = e.astype(bf16)
            new_total = jnp.sum(e, axis=0, keepdims=True)
            new_acc = mm(valuesT, eb)
            if not own:
                shrink = jnp.exp2((old[i][0] - new_top) * LOG2_SCALE)
                new_total = old[i][1] * shrink + new_total
                new_acc = old[i][2] * shrink + new_acc
            new.append((new_top, new_total, new_acc, eb))
        for s, (new_top, new_total, new_acc, eb) in zip(cols, new):
            top[:, s] = new_top
            total[:, s] = new_total
            acc[:, s] = new_acc
            E[d, :, s] = eb
            block_top[pl.ds(d, 1), s] = new_top

    pass_x(0)
    for d in (7, 6, 5):

        @when(plane + d == LAST)
        def _():
            send_w(d, 0, LAST).start()

    @when(plane == LAST)
    def _():
        pass_z(3)
        pass_z(4)

    pass_z(1)
    pass_z(2)
    relay()
    forward(0, True)

    ahead = jnp.where(plane == LAST, LAST - 1, Z_AHEAD)

    @pl.loop(jnp.where(plane == LAST, 5, 3), ahead + 1)
    def _(i):
        pass_z(i)

    pass_x(1)

    @pl.loop(1, plane + 1)
    def _(i):
        pass_z(i + ahead)
        pass_x(i + 1)
        forward(block_at(i), False)

    ob = (acc[...] / total[...]).astype(bf16)
    outT[...] = ob
    for h in range(HEADS):
        s = slice(h * TOK, (h + 1) * TOK)
        out[:, s] = ob[:, s].T
    store_out[0].start()
    dqT[...] = jnp.zeros_like(dqT)

    def join_core(d):
        grad_core(d).wait_recv()
        for j in range(2):
            H[d, j] = (G[d, core, j].astype(f32) + from_core[d, j].astype(f32)).astype(bf16)

    def pass_core(d):
        join_core(d)

        grad_x(d).start()

    def join_x(d):
        grad_x(d).wait_recv()
        Z[d] = (H[d, x].astype(f32) + from_x[d].astype(f32)).astype(bf16)

    def join_z():
        for d in (4, 3):

            @when((plane >= 2) & (plane + d - 2 < PLANES))
            def _():
                grad_z(d).wait_recv()
                Z[2] = (Z[2].astype(f32) + from_z[d].astype(f32)).astype(bf16)

    def nth(step):
        return jnp.where((plane == LAST) & (step < 3), 5 + step, plane - step)

    @pl.loop(0, plane + 1)
    def _(step):
        d = nth(step)
        c = jnp.exp2((block_top[pl.ds(d, 1), :] - top[...]) * LOG2_SCALE) / total[...]
        gc = (gT[...].astype(f32) * c).astype(bf16)
        delta = jnp.sum(gc.astype(f32) * outT[...].astype(f32), axis=0, keepdims=True)
        dP = mm(values_of(d), gc)
        e = E[d]
        dS = (e.astype(f32) * (dP - delta)).astype(bf16)
        dqT[...] += mm(keys_of(d).T, dS)
        dk = mm_nt(qT[...], dS).astype(bf16)
        dv = mm_nt(gc, e).astype(bf16)
        for j in range(QUAD):
            G[d, j // 2, j % 2, :HD, :] = dk[:, j * TOK : (j + 1) * TOK]
            G[d, j // 2, j % 2, HD:, :] = dv[:, j * TOK : (j + 1) * TOK]
        grad_core(d).start()

        @when(step >= 1)
        def _():
            pass_core(nth(step - 1))

        @when(step >= X_AHEAD)
        def _():
            done = nth(step - X_AHEAD)
            join_x(done)
            grad_z(done).start()

    join_core(0)

    grad_x(0).start()

    for d in range(X_AHEAD - 1, 2, -1):

        @when(d <= plane)
        def _():
            join_x(d)
            grad_z(d).start()

    @when(plane >= 1)
    def _():
        @when(plane >= 2)
        def _():
            join_x(2)

        join_x(1)
        grad_z(1).start()

    @when(plane >= 2)
    def _():
        join_z()
        grad_z(2).start()

    for h in range(HEADS):
        s = slice(h * TOK, (h + 1) * TOK)
        dq[:, s] = (dqT[:, s] * SCALE).astype(bf16).T
    store_out[1].start()
    join_x(0)
    dqT[:, : 2 * HD] = Z[0].astype(f32).reshape(2, HD, TOK).transpose(1, 0, 2).reshape(HD, 2 * HD)

    for d in (5, 6, 7, 1, 2):

        @when(plane + d < PLANES)
        def _():
            grad_z(d).wait_recv()
            more = from_z[d].astype(f32)
            dqT[:, :HD] += more[:HD]
            dqT[:, HD : 2 * HD] += more[HD:]

    dk_out[...] = (dqT[:, :HD] * SCALE).T.astype(bf16)
    dv_out[...] = dqT[:, HD : 2 * HD].T.astype(bf16)

    store_out[2].start()
    store_out[3].start()

    @pl.loop(0, plane + 1)
    def _(d):
        send_core(d, 0).wait_send()
        send_core(d, 1).wait_send()
        grad_core(d).wait_send()

        grad_x(d).wait_send()

        @when(narrow(d))
        def _():
            send_x(d).wait_send()

        @when(d >= 1)
        def _():
            grad_z(d).wait_send()

    for d in range(1, PLANES):

        @when(direct(d))
        def _():
            send_own(d).wait_send()

        if d >= 5:

            @when(plane + d == LAST)
            def _():
                send_w(d, 0, LAST).wait_send()

    for d in (3, 4):

        @when(relayed(d))
        def _():
            relay_up(d).wait_send()

    @when(plane == LAST)
    def _():
        for i in range(3):
            round_own(i).wait_send()

    for m in store_out:
        m.wait()


def deliver(*refs):
    moves = [pltpu.make_async_copy(refs[i], refs[4 + i], refs[8].at[i]) for i in range(4)]
    for m in moves:
        m.start()
    for m in moves:
        m.wait()


def local(queries, keys, values, out_grad):
    dma = pltpu.SemaphoreType.DMA
    shapes = [
        jax.ShapeDtypeStruct((TOK, ROWS), bf16),
        jax.ShapeDtypeStruct((TOK, ROWS), bf16),
        jax.ShapeDtypeStruct((TOK, HD), bf16),
        jax.ShapeDtypeStruct((TOK, HD), bf16),
    ]
    results = pl.pallas_call(
        attend,
        out_shape=shapes,
        in_specs=[pl.BlockSpec(memory_space=pltpu.HBM)] * 4,
        out_specs=[pl.BlockSpec(memory_space=pltpu.HBM)] * 4,
        scratch_shapes=[
            pltpu.VMEM((TOK, ROWS), bf16),
            pltpu.VMEM((TOK, ROWS), bf16),
            pltpu.VMEM((TOK, HD), bf16),
            pltpu.VMEM((TOK, HD), bf16),
            pltpu.VMEM((TOK, ROWS), bf16),
            pltpu.VMEM((TOK, ROWS), bf16),
            pltpu.VMEM((TOK, HD), bf16),
            pltpu.VMEM((TOK, HD), bf16),
            pltpu.VMEM((PLANES, 2, 2, TOK, 2 * HD), bf16),
            pltpu.VMEM((HD, ROWS), bf16),
            pltpu.VMEM((HD, ROWS), bf16),
            pltpu.VMEM((PLANES, KEYS, ROWS), bf16),
            pltpu.VMEM((1, ROWS), f32),
            pltpu.VMEM((1, ROWS), f32),
            pltpu.VMEM((PLANES, ROWS), f32),
            pltpu.VMEM((HD, ROWS), f32),
            pltpu.VMEM((HD, ROWS), bf16),
            pltpu.VMEM((HD, ROWS), f32),
            pltpu.VMEM((PLANES, 2, 2, 2 * HD, TOK), bf16),
            pltpu.VMEM((PLANES, 2, 2 * HD, TOK), bf16),
            pltpu.VMEM((PLANES, 2, 2 * HD, TOK), bf16),
            pltpu.VMEM((PLANES, 2 * HD, TOK), bf16),
            pltpu.VMEM((PLANES, 2 * HD, TOK), bf16),
            pltpu.VMEM((PLANES, 2 * HD, TOK), bf16),
        ]
        + [dma((4,))] * 2
        + [dma((PLANES,))] * 6
        + [dma((PLANES, 2))] * 2
        + [dma((PLANES,))] * 6,
        compiler_params=pltpu.CompilerParams(
            collective_id=0, has_side_effects=True, vmem_limit_bytes=62 << 20
        ),
    )(queries, out_grad, keys, values)
    return pl.pallas_call(
        deliver,
        out_shape=shapes,
        in_specs=[pl.BlockSpec(memory_space=pltpu.VMEM)] * 4,
        out_specs=[pl.BlockSpec(memory_space=pltpu.HBM)] * 4,
        scratch_shapes=[dma((4,))],
        compiler_params=pltpu.CompilerParams(vmem_limit_bytes=62 << 20),
    )(*results)


def solution(mesh):
    spec = P("ctx", "head")
    return jax.shard_map(local, mesh=mesh, in_specs=(spec,) * 4, out_specs=(spec,) * 4, check_vma=False)
```

```python
import math

import jax
import jax.numpy as jnp
from jax import lax
from jax.experimental import pallas as pl
from jax.experimental.pallas import tpu as pltpu
from jax.sharding import PartitionSpec as P

HEADS, HD, TOK, PLANES, QUAD = 8, 128, 128, 8, 4
KEYS, ROWS = QUAD * TOK, HEADS * TOK
SCALE = HD**-0.5
LOG2_SCALE = SCALE * math.log2(math.e)
X_AHEAD = 3
CHUNK = 256
Z_AHEAD = 3
LAST = PLANES - 1
f32, bf16 = jnp.float32, jnp.bfloat16


def mm(a, b):
    return jnp.dot(a, b, preferred_element_type=f32)


def mm_nt(a, b):
    return lax.dot_general(a, b, (((1,), (1,)), ((), ())), preferred_element_type=f32)


def when(condition):
    return pl.when(condition)


def attend(
    q_hbm, g_hbm, k_hbm, v_hbm, out_hbm, dq_hbm, dk_hbm, dv_hbm,
    q, g, k, v, out, dq, dk_out, dv_out, kv, qT, gT, E, top, total, block_top, acc, outT, dqT,
    G, from_core, H, from_x, Z, from_z, from_w,
    load, store, z_out, z_in, w_out, w_in, x_out, x_in, c_out, c_in, gc_out, gc_in, gx_out, gx_in, gz_out, gz_in, gw_out, gw_in,
):
    me, head = lax.axis_index("ctx"), lax.axis_index("head")
    plane, place = me // QUAD, me % QUAD
    x, core = place // 2, place % 2

    def at(z, x_, core_):
        return dict(device_id=(z * QUAD + x_ * 2 + core_, head), device_id_type=pl.DeviceIdType.MESH)

    def shard(d, core_, x_):
        return kv.at[d, core_, x_]

    def copy(src, dst, s, r, where):
        return pltpu.make_async_remote_copy(src, dst, s, r, **where)

    def send_z(d, src, hops):
        return copy(shard(src, core, x), shard(d, core, x), z_out.at[d], z_in.at[d], at(lax.rem(plane + hops, PLANES), x, core))

    def send_w(d, src, to):
        return copy(shard(src, core, 1 - x), shard(d, core, 1 - x), w_out.at[d], w_in.at[d], at(to, x, core))

    def get_z(d):
        return copy(shard(d, core, x), shard(d, core, x), z_out.at[d], z_in.at[d], at(plane, x, 1 - core))

    def get_w(d):
        return copy(shard(d, core, 1 - x), shard(d, core, 1 - x), w_out.at[d], w_in.at[d], at(plane, x, 1 - core))

    def narrow(d):
        return (d <= 4) | (plane != LAST)

    def direct(d):
        return ((d <= 2) & (plane + d <= LAST)) | ((d >= 5) & (plane + d == LAST))

    def relayed(d):
        return (plane >= 2) & (plane + d - 2 <= LAST)

    def send_own(d):
        return send_z(d, 0, d)

    def relay_up(d):
        return send_z(d, 2, d - 2)

    ROUND = ((6, 7, LAST - 1), (5, 7, LAST - 2), (5, 6, LAST - 1))

    def round_own(i):
        d, src, to = ROUND[i]
        return copy(shard(src, core, x), shard(d, core, x), z_out.at[i], z_in.at[d], at(to, x, core))

    def relay_round(d):
        @when((plane == LAST) & (d == LAST))
        def _():
            round_own(0).start()
            round_own(1).start()

        @when((plane == LAST) & (d == LAST - 1))
        def _():
            round_own(2).start()

    def send_x(d):
        return copy(shard(d, core, x), shard(d, core, x), x_out.at[d], x_in.at[d], at(plane, 1 - x, core))

    def get_x(d):
        return copy(shard(d, core, 1 - x), shard(d, core, 1 - x), x_out.at[d], x_in.at[d], at(plane, 1 - x, core))

    def send_core(d, j):
        which = x if j == 0 else 1 - x
        return copy(shard(d, core, which), shard(d, core, which), c_out.at[d, j], c_in.at[d, j], at(plane, x, 1 - core))

    def get_core(d, j):
        which = x if j == 0 else 1 - x
        return copy(shard(d, 1 - core, which), shard(d, 1 - core, which), c_out.at[d, j], c_in.at[d, j], at(plane, x, 1 - core))

    def grad_core(d):
        return copy(G.at[d, 1 - core], from_core.at[d], gc_out.at[d], gc_in.at[d], at(plane, x, 1 - core))

    def grad_x(d):
        return copy(H.at[d, 1 - x], from_x.at[d], gx_out.at[d], gx_in.at[d], at(plane, 1 - x, core))

    def grad_z(d):
        hops = jnp.where((d == 3) | (d == 4), d - 2, d)
        return copy(Z.at[d], from_z.at[d], gz_out.at[d], gz_in.at[d], at(lax.rem(plane + PLANES - hops, PLANES), x, core))

    def wide(d):
        return (plane == LAST) & (d == 5)

    def grad_w():
        return copy(H.at[5], from_w, gw_out, gw_in, at(LAST - 5, x, core))

    wraps = jnp.maximum(plane - 4, 0)

    def block_at(i):
        return jnp.where(i <= 2, i, jnp.where(i < 3 + wraps, plane + 3 - i, i - wraps))

    fetch = [
        pltpu.make_async_copy(src, dst, load.at[i])
        for i, (src, dst) in enumerate(
            ((k_hbm, k), (v_hbm, v), (q_hbm, q), (g_hbm, g))
        )
    ]
    store_out = [
        pltpu.make_async_copy(src, dst, store.at[i])
        for i, (src, dst) in enumerate(
            ((out, out_hbm), (dq, dq_hbm), (dk_out, dk_hbm), (dv_out, dv_hbm))
        )
    ]
    for f in fetch:
        f.start()
    barrier = pltpu.get_barrier_semaphore()

    def greet(where):
        pl.semaphore_signal(barrier, inc=1, **where)

    greet(at(plane, x, 1 - core))
    greet(at(plane, 1 - x, core))
    for d in range(1, PLANES):
        greet(at(lax.rem(plane + d, PLANES), x, core))
    fetch[0].wait()
    fetch[1].wait()
    kv[0, core, x, :, :HD] = k[...]
    kv[0, core, x, :, HD:] = v[...]
    pl.semaphore_wait(barrier, PLANES + 1)

    send_core(0, 0).start()
    send_x(0).start()
    for d in (7, 6, 5, 4, 3, 2, 1):

        @when(direct(d))
        def _():
            send_own(d).start()

    fetch[2].wait()
    fetch[3].wait()
    for h in range(HEADS):
        s = slice(h * TOK, (h + 1) * TOK)
        qT[:, s] = q[:, s].T
        gT[:, s] = g[:, s].T

    def pass_z(i):
        @when(i <= plane)
        def _():
            d = block_at(i)
            get_z(d).wait_recv()
            relay_round(d)

            @when(narrow(d))
            def _():
                send_x(d).start()

            send_core(d, 0).start()

    def relay():
        for d in (4, 3):

            @when(relayed(d))
            def _():
                relay_up(d).start()

    def pass_x(i):
        @when(i <= plane)
        def _():
            d = block_at(i)

            @when(narrow(d))
            def _():
                get_x(d).wait_recv()

            @when(~narrow(d))
            def _():
                get_w(d).wait_recv()

            send_core(d, 1).start()

    def keys_of(d):
        return kv[d, :, :, :, :HD].reshape(KEYS, HD)

    def values_of(d):
        return kv[d, :, :, :, HD:].reshape(KEYS, HD)

    def forward(d, own):
        get_core(d, 0).wait_recv()
        get_core(d, 1).wait_recv()
        cols = [slice(i * CHUNK, (i + 1) * CHUNK) for i in range(ROWS // CHUNK)]
        old = [None if own else (top[:, s], total[:, s], acc[:, s]) for s in cols]
        keys_d, valuesT = keys_of(d), values_of(d).T
        scores = [mm(keys_d, qT[:, s]) for s in cols]
        if own:
            row = lax.broadcasted_iota(jnp.int32, (KEYS, CHUNK), 0)
            key_at = ((row // TOK) % 2) * (2 * TOK) + (row // (2 * TOK)) * TOK + (row & (TOK - 1))
            query_at = place * TOK + (lax.broadcasted_iota(jnp.int32, (KEYS, CHUNK), 1) & (TOK - 1))
            visible = key_at <= query_at
        new = []
        for i, S in enumerate(scores):
            if own:
                S = jnp.where(visible, S, -1e30)
            new_top = jnp.max(S, axis=0, keepdims=True)
            if not own:
                new_top = jnp.maximum(old[i][0], new_top)
            e = jnp.exp2((S - new_top) * LOG2_SCALE)
            if own:
                e = jnp.where(visible, e, 0.0)
            eb = e.astype(bf16)
            new_total = jnp.sum(e, axis=0, keepdims=True)
            new_acc = mm(valuesT, eb)
            if not own:
                shrink = jnp.exp2((old[i][0] - new_top) * LOG2_SCALE)
                new_total = old[i][1] * shrink + new_total
                new_acc = old[i][2] * shrink + new_acc
            new.append((new_top, new_total, new_acc, eb))
        for s, (new_top, new_total, new_acc, eb) in zip(cols, new):
            top[:, s] = new_top
            total[:, s] = new_total
            acc[:, s] = new_acc
            E[d, :, s] = eb
            block_top[pl.ds(d, 1), s] = new_top

    pass_x(0)
    for d in (7, 6, 5):

        @when(plane + d == LAST)
        def _():
            send_w(d, 0, LAST).start()

    @when(plane == LAST)
    def _():
        pass_z(3)
        pass_z(4)

    pass_z(1)
    pass_z(2)
    relay()
    forward(0, True)

    ahead = jnp.where(plane == LAST, LAST - 1, Z_AHEAD)

    @pl.loop(jnp.where(plane == LAST, 5, 3), ahead + 1)
    def _(i):
        pass_z(i)

    pass_x(1)

    @pl.loop(1, plane + 1)
    def _(i):
        pass_z(i + ahead)
        pass_x(i + 1)
        forward(block_at(i), False)

    ob = (acc[...] / total[...]).astype(bf16)
    outT[...] = ob
    for h in range(HEADS):
        s = slice(h * TOK, (h + 1) * TOK)
        out[:, s] = ob[:, s].T
    store_out[0].start()
    dqT[...] = jnp.zeros_like(dqT)

    def join_core(d):
        grad_core(d).wait_recv()
        for j in range(2):
            H[d, j] = (G[d, core, j].astype(f32) + from_core[d, j].astype(f32)).astype(bf16)

    def pass_core(d):
        join_core(d)

        @when(wide(d))
        def _():
            grad_w().start()

        @when(jnp.logical_not(wide(d)))
        def _():
            grad_x(d).start()

    def join_x(d):
        grad_x(d).wait_recv()
        Z[d] = (H[d, x].astype(f32) + from_x[d].astype(f32)).astype(bf16)

    def join_z():
        for d in (4, 3):

            @when((plane >= 2) & (plane + d - 2 < PLANES))
            def _():
                grad_z(d).wait_recv()
                Z[2] = (Z[2].astype(f32) + from_z[d].astype(f32)).astype(bf16)

    def nth(step):
        last = jnp.where(step == 0, 5, jnp.where(step == 1, 7, jnp.where(step == 2, 6, jnp.where(step == 3, 4, plane - step))))
        second = jnp.where(step == 0, 4, jnp.where(step == 1, 3, jnp.where(step == 2, 6, jnp.where(step == 3, 5, plane - step))))
        return jnp.where(plane == LAST, last, jnp.where(plane == LAST - 1, second, block_at(plane - step)))

    @pl.loop(0, plane + 1)
    def _(step):
        d = nth(step)
        c = jnp.exp2((block_top[pl.ds(d, 1), :] - top[...]) * LOG2_SCALE) / total[...]
        gc = (gT[...].astype(f32) * c).astype(bf16)
        delta = jnp.sum(gc.astype(f32) * outT[...].astype(f32), axis=0, keepdims=True)
        dP = mm(values_of(d), gc)
        e = E[d]
        dS = (e.astype(f32) * (dP - delta)).astype(bf16)
        dqT[...] += mm(keys_of(d).T, dS)
        dk = mm_nt(qT[...], dS).astype(bf16)
        dv = mm_nt(gc, e).astype(bf16)
        for j in range(QUAD):
            G[d, j // 2, j % 2, :HD, :] = dk[:, j * TOK : (j + 1) * TOK]
            G[d, j // 2, j % 2, HD:, :] = dv[:, j * TOK : (j + 1) * TOK]
        grad_core(d).start()

        @when(step >= 1)
        def _():
            pass_core(nth(step - 1))

        @when(step >= X_AHEAD)
        def _():
            done = nth(step - X_AHEAD)

            @when(jnp.logical_not(wide(done)))
            def _():
                join_x(done)
                grad_z(done).start()

    join_core(0)

    @when(plane != LAST - 5)
    def _():
        grad_x(0).start()

    for d in range(X_AHEAD - 1, 2, -1):

        @when(d <= plane)
        def _():
            join_x(d)
            grad_z(d).start()

    @when(plane >= 1)
    def _():
        @when(plane >= 2)
        def _():
            join_x(2)

        join_x(1)
        grad_z(1).start()

    @when(plane >= 2)
    def _():
        join_z()
        grad_z(2).start()

    @when(plane == LAST - 5)
    def _():
        copy(H.at[0], from_w, gw_out, gw_in, at(plane, x, 1 - core)).wait_recv()
        H[0] = (H[0].astype(f32) + from_w[...].astype(f32)).astype(bf16)
        grad_x(0).start()

    for h in range(HEADS):
        s = slice(h * TOK, (h + 1) * TOK)
        dq[:, s] = (dqT[:, s] * SCALE).astype(bf16).T
    store_out[1].start()
    join_x(0)
    dqT[:, : 2 * HD] = Z[0].astype(f32).reshape(2, HD, TOK).transpose(1, 0, 2).reshape(HD, 2 * HD)

    for d in (5, 6, 7, 1, 2):

        @when(plane + d < (LAST if d == 5 else PLANES))
        def _():
            grad_z(d).wait_recv()
            more = from_z[d].astype(f32)
            dqT[:, :HD] += more[:HD]
            dqT[:, HD : 2 * HD] += more[HD:]

    dk_out[...] = (dqT[:, :HD] * SCALE).T.astype(bf16)
    dv_out[...] = dqT[:, HD : 2 * HD].T.astype(bf16)

    store_out[2].start()
    store_out[3].start()

    @pl.loop(0, plane + 1)
    def _(d):
        send_core(d, 0).wait_send()
        send_core(d, 1).wait_send()
        grad_core(d).wait_send()


        @when(narrow(d))
        def _():
            send_x(d).wait_send()

        @when(wide(d))
        def _():
            grad_w().wait_send()

        @when(jnp.logical_not(wide(d)))
        def _():
            grad_x(d).wait_send()

            @when(d >= 1)
            def _():
                grad_z(d).wait_send()

    for d in range(1, PLANES):

        @when(direct(d))
        def _():
            send_own(d).wait_send()

        if d >= 5:

            @when(plane + d == LAST)
            def _():
                send_w(d, 0, LAST).wait_send()

    for d in (3, 4):

        @when(relayed(d))
        def _():
            relay_up(d).wait_send()

    @when(plane == LAST)
    def _():
        for i in range(3):
            round_own(i).wait_send()

    for m in store_out:
        m.wait()


def deliver(*refs):
    moves = [pltpu.make_async_copy(refs[i], refs[4 + i], refs[8].at[i]) for i in range(4)]
    for m in moves:
        m.start()
    for m in moves:
        m.wait()


def local(queries, keys, values, out_grad):
    dma = pltpu.SemaphoreType.DMA
    shapes = [
        jax.ShapeDtypeStruct((TOK, ROWS), bf16),
        jax.ShapeDtypeStruct((TOK, ROWS), bf16),
        jax.ShapeDtypeStruct((TOK, HD), bf16),
        jax.ShapeDtypeStruct((TOK, HD), bf16),
    ]
    results = pl.pallas_call(
        attend,
        out_shape=shapes,
        in_specs=[pl.BlockSpec(memory_space=pltpu.HBM)] * 4,
        out_specs=[pl.BlockSpec(memory_space=pltpu.HBM)] * 4,
        scratch_shapes=[
            pltpu.VMEM((TOK, ROWS), bf16),
            pltpu.VMEM((TOK, ROWS), bf16),
            pltpu.VMEM((TOK, HD), bf16),
            pltpu.VMEM((TOK, HD), bf16),
            pltpu.VMEM((TOK, ROWS), bf16),
            pltpu.VMEM((TOK, ROWS), bf16),
            pltpu.VMEM((TOK, HD), bf16),
            pltpu.VMEM((TOK, HD), bf16),
            pltpu.VMEM((PLANES, 2, 2, TOK, 2 * HD), bf16),
            pltpu.VMEM((HD, ROWS), bf16),
            pltpu.VMEM((HD, ROWS), bf16),
            pltpu.VMEM((PLANES, KEYS, ROWS), bf16),
            pltpu.VMEM((1, ROWS), f32),
            pltpu.VMEM((1, ROWS), f32),
            pltpu.VMEM((PLANES, ROWS), f32),
            pltpu.VMEM((HD, ROWS), f32),
            pltpu.VMEM((HD, ROWS), bf16),
            pltpu.VMEM((HD, ROWS), f32),
            pltpu.VMEM((PLANES, 2, 2, 2 * HD, TOK), bf16),
            pltpu.VMEM((PLANES, 2, 2 * HD, TOK), bf16),
            pltpu.VMEM((PLANES, 2, 2 * HD, TOK), bf16),
            pltpu.VMEM((PLANES, 2 * HD, TOK), bf16),
            pltpu.VMEM((PLANES, 2 * HD, TOK), bf16),
            pltpu.VMEM((PLANES, 2 * HD, TOK), bf16),
            pltpu.VMEM((2, 2 * HD, TOK), bf16),
        ]
        + [dma((4,))] * 2
        + [dma((PLANES,))] * 6
        + [dma((PLANES, 2))] * 2
        + [dma((PLANES,))] * 6
        + [dma] * 2,
        compiler_params=pltpu.CompilerParams(
            collective_id=0, has_side_effects=True, vmem_limit_bytes=62 << 20
        ),
    )(queries, out_grad, keys, values)
    return pl.pallas_call(
        deliver,
        out_shape=shapes,
        in_specs=[pl.BlockSpec(memory_space=pltpu.VMEM)] * 4,
        out_specs=[pl.BlockSpec(memory_space=pltpu.HBM)] * 4,
        scratch_shapes=[dma((4,))],
        compiler_params=pltpu.CompilerParams(vmem_limit_bytes=62 << 20),
    )(*results)


def solution(mesh):
    spec = P("ctx", "head")
    return jax.shard_map(local, mesh=mesh, in_specs=(spec,) * 4, out_specs=(spec,) * 4, check_vma=False)
```

```python
import math

import jax
import jax.numpy as jnp
from jax import lax
from jax.experimental import pallas as pl
from jax.experimental.pallas import tpu as pltpu
from jax.sharding import PartitionSpec as P

HEADS, HD, TOK, PLANES, QUAD = 8, 128, 128, 8, 4
KEYS, ROWS = QUAD * TOK, HEADS * TOK
SCALE = HD**-0.5
LOG2_SCALE = SCALE * math.log2(math.e)
X_AHEAD = 3
CHUNK = 256
Z_AHEAD = 3
LAST = PLANES - 1
f32, bf16 = jnp.float32, jnp.bfloat16


def mm(a, b):
    return jnp.dot(a, b, preferred_element_type=f32)


def mm_nt(a, b):
    return lax.dot_general(a, b, (((1,), (1,)), ((), ())), preferred_element_type=f32)


def when(condition):
    return pl.when(condition)


def attend(
    q_hbm, g_hbm, k_hbm, v_hbm, out_hbm, dq_hbm, dk_hbm, dv_hbm,
    q, g, k, v, out, dq, dk_out, dv_out, kv, qT, gT, E, top, total, block_top, acc, outT, dqT,
    G, from_core, H, from_x, Z, from_z, from_w,
    load, store, z_out, z_in, w_out, w_in, x_out, x_in, c_out, c_in, gc_out, gc_in, gx_out, gx_in, gz_out, gz_in, gw_out, gw_in,
):
    me, head = lax.axis_index("ctx"), lax.axis_index("head")
    plane, place = me // QUAD, me % QUAD
    x, core = place // 2, place % 2

    def at(z, x_, core_):
        return dict(device_id=(z * QUAD + x_ * 2 + core_, head), device_id_type=pl.DeviceIdType.MESH)

    def shard(d, core_, x_):
        return kv.at[d, core_, x_]

    def copy(src, dst, s, r, where):
        return pltpu.make_async_remote_copy(src, dst, s, r, **where)

    def send_z(d, src, hops):
        return copy(shard(src, core, x), shard(d, core, x), z_out.at[d], z_in.at[d], at(lax.rem(plane + hops, PLANES), x, core))

    def send_w(d, src, to):
        return copy(shard(src, core, 1 - x), shard(d, core, 1 - x), w_out.at[d], w_in.at[d], at(to, x, core))

    def get_z(d):
        return copy(shard(d, core, x), shard(d, core, x), z_out.at[d], z_in.at[d], at(plane, x, 1 - core))

    def get_w(d):
        return copy(shard(d, core, 1 - x), shard(d, core, 1 - x), w_out.at[d], w_in.at[d], at(plane, x, 1 - core))

    def narrow(d):
        return (d <= 4) | (plane != LAST)

    def direct(d):
        return ((d <= 2) & (plane + d <= LAST)) | ((d >= 5) & (plane + d == LAST))

    def relayed(d):
        return (plane >= 2) & (plane + d - 2 <= LAST)

    def send_own(d):
        return send_z(d, 0, d)

    def relay_up(d):
        return send_z(d, 2, d - 2)

    ROUND = ((6, 7, LAST - 1), (5, 7, LAST - 2), (5, 6, LAST - 1))

    def round_own(i):
        d, src, to = ROUND[i]
        return copy(shard(src, core, x), shard(d, core, x), z_out.at[i], z_in.at[d], at(to, x, core))

    def relay_round(d):
        @when((plane == LAST) & (d == LAST))
        def _():
            round_own(0).start()
            round_own(1).start()

        @when((plane == LAST) & (d == LAST - 1))
        def _():
            round_own(2).start()

    def send_x(d):
        return copy(shard(d, core, x), shard(d, core, x), x_out.at[d], x_in.at[d], at(plane, 1 - x, core))

    def get_x(d):
        return copy(shard(d, core, 1 - x), shard(d, core, 1 - x), x_out.at[d], x_in.at[d], at(plane, 1 - x, core))

    def send_core(d, j):
        which = x if j == 0 else 1 - x
        return copy(shard(d, core, which), shard(d, core, which), c_out.at[d, j], c_in.at[d, j], at(plane, x, 1 - core))

    def get_core(d, j):
        which = x if j == 0 else 1 - x
        return copy(shard(d, 1 - core, which), shard(d, 1 - core, which), c_out.at[d, j], c_in.at[d, j], at(plane, x, 1 - core))

    def grad_core(d):
        return copy(G.at[d, 1 - core], from_core.at[d], gc_out.at[d], gc_in.at[d], at(plane, x, 1 - core))

    def grad_x(d):
        return copy(H.at[d, 1 - x], from_x.at[d], gx_out.at[d], gx_in.at[d], at(plane, 1 - x, core))

    def grad_z(d):
        hops = jnp.where((d == 3) | (d == 4), d - 2, d)
        return copy(Z.at[d], from_z.at[d], gz_out.at[d], gz_in.at[d], at(lax.rem(plane + PLANES - hops, PLANES), x, core))

    def wide(d):
        return (plane == LAST) & (d == 5)

    def grad_w():
        return copy(H.at[5], from_w, gw_out, gw_in, at(LAST - 5, x, core))

    wraps = jnp.maximum(plane - 4, 0)

    def block_at(i):
        return jnp.where(i <= 2, i, jnp.where(i < 3 + wraps, plane + 3 - i, i - wraps))

    fetch = [
        pltpu.make_async_copy(src, dst, load.at[i])
        for i, (src, dst) in enumerate(
            ((k_hbm, k), (v_hbm, v), (q_hbm, q), (g_hbm, g))
        )
    ]
    store_out = [
        pltpu.make_async_copy(src, dst, store.at[i])
        for i, (src, dst) in enumerate(
            ((out, out_hbm), (dq, dq_hbm), (dk_out, dk_hbm), (dv_out, dv_hbm))
        )
    ]
    for f in fetch:
        f.start()
    barrier = pltpu.get_barrier_semaphore()

    def greet(where):
        pl.semaphore_signal(barrier, inc=1, **where)

    greet(at(plane, x, 1 - core))
    greet(at(plane, 1 - x, core))
    for d in (1, 2, PLANES - 2, PLANES - 1):
        greet(at(lax.rem(plane + d, PLANES), x, core))
    partners = jnp.where((plane < 3) | (plane > 4), 7, 6)

    @when(plane < 3)
    def _():
        greet(at(plane + 5, x, core))

    @when(plane > 4)
    def _():
        greet(at(plane - 5, x, core))

    fetch[0].wait()
    fetch[1].wait()
    kv[0, core, x, :, :HD] = k[...]
    kv[0, core, x, :, HD:] = v[...]
    pl.semaphore_wait(barrier, partners)

    send_core(0, 0).start()
    send_x(0).start()
    for d in (7, 6, 5, 4, 3, 2, 1):

        @when(direct(d))
        def _():
            send_own(d).start()

    fetch[2].wait()
    fetch[3].wait()
    for h in range(HEADS):
        s = slice(h * TOK, (h + 1) * TOK)
        qT[:, s] = q[:, s].T
        gT[:, s] = g[:, s].T

    def pass_z(i):
        @when(i <= plane)
        def _():
            d = block_at(i)
            get_z(d).wait_recv()
            relay_round(d)

            @when(narrow(d))
            def _():
                send_x(d).start()

            send_core(d, 0).start()

    def relay():
        for d in (4, 3):

            @when(relayed(d))
            def _():
                relay_up(d).start()

    def pass_x(i):
        @when(i <= plane)
        def _():
            d = block_at(i)

            @when(narrow(d))
            def _():
                get_x(d).wait_recv()

            @when(~narrow(d))
            def _():
                get_w(d).wait_recv()

            send_core(d, 1).start()

    def keys_of(d):
        return kv[d, :, :, :, :HD].reshape(KEYS, HD)

    def values_of(d):
        return kv[d, :, :, :, HD:].reshape(KEYS, HD)

    def forward(d, own):
        get_core(d, 0).wait_recv()
        get_core(d, 1).wait_recv()
        cols = [slice(i * CHUNK, (i + 1) * CHUNK) for i in range(ROWS // CHUNK)]
        old = [None if own else (top[:, s], total[:, s], acc[:, s]) for s in cols]
        keys_d, valuesT = keys_of(d), values_of(d).T
        scores = [mm(keys_d, qT[:, s]) for s in cols]
        if own:
            row = lax.broadcasted_iota(jnp.int32, (KEYS, CHUNK), 0)
            key_at = ((row // TOK) % 2) * (2 * TOK) + (row // (2 * TOK)) * TOK + (row & (TOK - 1))
            query_at = place * TOK + (lax.broadcasted_iota(jnp.int32, (KEYS, CHUNK), 1) & (TOK - 1))
            visible = key_at <= query_at
        new = []
        for i, S in enumerate(scores):
            if own:
                S = jnp.where(visible, S, -1e30)
            new_top = jnp.max(S, axis=0, keepdims=True)
            if not own:
                new_top = jnp.maximum(old[i][0], new_top)
            e = jnp.exp2((S - new_top) * LOG2_SCALE)
            if own:
                e = jnp.where(visible, e, 0.0)
            eb = e.astype(bf16)
            new_total = jnp.sum(e, axis=0, keepdims=True)
            new_acc = mm(valuesT, eb)
            if not own:
                shrink = jnp.exp2((old[i][0] - new_top) * LOG2_SCALE)
                new_total = old[i][1] * shrink + new_total
                new_acc = old[i][2] * shrink + new_acc
            new.append((new_top, new_total, new_acc, eb))
        for s, (new_top, new_total, new_acc, eb) in zip(cols, new):
            top[:, s] = new_top
            total[:, s] = new_total
            acc[:, s] = new_acc
            E[d, :, s] = eb
            block_top[pl.ds(d, 1), s] = new_top

    pass_x(0)
    for d in (7, 6, 5):

        @when(plane + d == LAST)
        def _():
            send_w(d, 0, LAST).start()

    @when(plane == LAST)
    def _():
        pass_z(3)
        pass_z(4)

    pass_z(1)
    pass_z(2)
    relay()
    forward(0, True)

    ahead = jnp.where(plane == LAST, LAST - 1, Z_AHEAD)

    @pl.loop(jnp.where(plane == LAST, 5, 3), ahead + 1)
    def _(i):
        pass_z(i)

    pass_x(1)

    @pl.loop(1, plane + 1)
    def _(i):
        pass_z(i + ahead)
        pass_x(i + 1)
        forward(block_at(i), False)

    ob = (acc[...] / total[...]).astype(bf16)
    outT[...] = ob
    for h in range(HEADS):
        s = slice(h * TOK, (h + 1) * TOK)
        out[:, s] = ob[:, s].T
    store_out[0].start()
    dqT[...] = jnp.zeros_like(dqT)

    def join_core(d):
        grad_core(d).wait_recv()
        for j in range(2):
            H[d, j] = (G[d, core, j].astype(f32) + from_core[d, j].astype(f32)).astype(bf16)

    def pass_core(d):
        join_core(d)

        @when(wide(d))
        def _():
            grad_w().start()

        @when(jnp.logical_not(wide(d)))
        def _():
            grad_x(d).start()

    def join_x(d):
        grad_x(d).wait_recv()
        Z[d] = (H[d, x].astype(f32) + from_x[d].astype(f32)).astype(bf16)

    def join_z():
        for d in (4, 3):

            @when((plane >= 2) & (plane + d - 2 < PLANES))
            def _():
                grad_z(d).wait_recv()
                Z[2] = (Z[2].astype(f32) + from_z[d].astype(f32)).astype(bf16)

    def nth(step):
        last = jnp.where(step == 0, 5, jnp.where(step == 1, 7, jnp.where(step == 2, 6, jnp.where(step == 3, 4, plane - step))))
        second = jnp.where(step == 0, 4, jnp.where(step == 1, 3, jnp.where(step == 2, 6, jnp.where(step == 3, 5, plane - step))))
        return jnp.where(plane == LAST, last, jnp.where(plane == LAST - 1, second, block_at(plane - step)))

    @pl.loop(0, plane + 1)
    def _(step):
        d = nth(step)
        c = jnp.exp2((block_top[pl.ds(d, 1), :] - top[...]) * LOG2_SCALE) / total[...]
        gc = (gT[...].astype(f32) * c).astype(bf16)
        delta = jnp.sum(gc.astype(f32) * outT[...].astype(f32), axis=0, keepdims=True)
        dP = mm(values_of(d), gc)
        e = E[d]
        dS = (e.astype(f32) * (dP - delta)).astype(bf16)
        dqT[...] += mm(keys_of(d).T, dS)
        dk = mm_nt(qT[...], dS).astype(bf16)
        dv = mm_nt(gc, e).astype(bf16)
        for j in range(QUAD):
            G[d, j // 2, j % 2, :HD, :] = dk[:, j * TOK : (j + 1) * TOK]
            G[d, j // 2, j % 2, HD:, :] = dv[:, j * TOK : (j + 1) * TOK]
        grad_core(d).start()

        @when(step >= 1)
        def _():
            pass_core(nth(step - 1))

        @when(step >= X_AHEAD)
        def _():
            done = nth(step - X_AHEAD)

            @when(jnp.logical_not(wide(done)))
            def _():
                join_x(done)
                grad_z(done).start()

    join_core(0)

    @when(plane != LAST - 5)
    def _():
        grad_x(0).start()

    for d in range(X_AHEAD - 1, 2, -1):

        @when(d <= plane)
        def _():
            join_x(d)
            grad_z(d).start()

    @when(plane >= 1)
    def _():
        @when(plane >= 2)
        def _():
            join_x(2)

        join_x(1)
        grad_z(1).start()

    @when(plane >= 2)
    def _():
        join_z()
        grad_z(2).start()

    @when(plane == LAST - 5)
    def _():
        copy(H.at[0], from_w, gw_out, gw_in, at(plane, x, 1 - core)).wait_recv()
        H[0] = (H[0].astype(f32) + from_w[...].astype(f32)).astype(bf16)
        grad_x(0).start()

    for h in range(HEADS):
        s = slice(h * TOK, (h + 1) * TOK)
        dq[:, s] = (dqT[:, s] * SCALE).astype(bf16).T
    store_out[1].start()
    join_x(0)
    dqT[:, : 2 * HD] = Z[0].astype(f32).reshape(2, HD, TOK).transpose(1, 0, 2).reshape(HD, 2 * HD)

    for d in (5, 6, 7, 1, 2):

        @when(plane + d < (LAST if d == 5 else PLANES))
        def _():
            grad_z(d).wait_recv()
            more = from_z[d].astype(f32)
            dqT[:, :HD] += more[:HD]
            dqT[:, HD : 2 * HD] += more[HD:]

    dk_out[...] = (dqT[:, :HD] * SCALE).T.astype(bf16)
    dv_out[...] = dqT[:, HD : 2 * HD].T.astype(bf16)

    store_out[2].start()
    store_out[3].start()

    @pl.loop(0, plane + 1)
    def _(d):
        send_core(d, 0).wait_send()
        send_core(d, 1).wait_send()
        grad_core(d).wait_send()


        @when(narrow(d))
        def _():
            send_x(d).wait_send()

        @when(wide(d))
        def _():
            grad_w().wait_send()

        @when(jnp.logical_not(wide(d)))
        def _():
            grad_x(d).wait_send()

            @when(d >= 1)
            def _():
                grad_z(d).wait_send()

    for d in range(1, PLANES):

        @when(direct(d))
        def _():
            send_own(d).wait_send()

        if d >= 5:

            @when(plane + d == LAST)
            def _():
                send_w(d, 0, LAST).wait_send()

    for d in (3, 4):

        @when(relayed(d))
        def _():
            relay_up(d).wait_send()

    @when(plane == LAST)
    def _():
        for i in range(3):
            round_own(i).wait_send()

    for m in store_out:
        m.wait()


def deliver(*refs):
    moves = [pltpu.make_async_copy(refs[i], refs[4 + i], refs[8].at[i]) for i in range(4)]
    for m in moves:
        m.start()
    for m in moves:
        m.wait()


def local(queries, keys, values, out_grad):
    dma = pltpu.SemaphoreType.DMA
    shapes = [
        jax.ShapeDtypeStruct((TOK, ROWS), bf16),
        jax.ShapeDtypeStruct((TOK, ROWS), bf16),
        jax.ShapeDtypeStruct((TOK, HD), bf16),
        jax.ShapeDtypeStruct((TOK, HD), bf16),
    ]
    results = pl.pallas_call(
        attend,
        out_shape=shapes,
        in_specs=[pl.BlockSpec(memory_space=pltpu.HBM)] * 4,
        out_specs=[pl.BlockSpec(memory_space=pltpu.HBM)] * 4,
        scratch_shapes=[
            pltpu.VMEM((TOK, ROWS), bf16),
            pltpu.VMEM((TOK, ROWS), bf16),
            pltpu.VMEM((TOK, HD), bf16),
            pltpu.VMEM((TOK, HD), bf16),
            pltpu.VMEM((TOK, ROWS), bf16),
            pltpu.VMEM((TOK, ROWS), bf16),
            pltpu.VMEM((TOK, HD), bf16),
            pltpu.VMEM((TOK, HD), bf16),
            pltpu.VMEM((PLANES, 2, 2, TOK, 2 * HD), bf16),
            pltpu.VMEM((HD, ROWS), bf16),
            pltpu.VMEM((HD, ROWS), bf16),
            pltpu.VMEM((PLANES, KEYS, ROWS), bf16),
            pltpu.VMEM((1, ROWS), f32),
            pltpu.VMEM((1, ROWS), f32),
            pltpu.VMEM((PLANES, ROWS), f32),
            pltpu.VMEM((HD, ROWS), f32),
            pltpu.VMEM((HD, ROWS), bf16),
            pltpu.VMEM((HD, ROWS), f32),
            pltpu.VMEM((PLANES, 2, 2, 2 * HD, TOK), bf16),
            pltpu.VMEM((PLANES, 2, 2 * HD, TOK), bf16),
            pltpu.VMEM((PLANES, 2, 2 * HD, TOK), bf16),
            pltpu.VMEM((PLANES, 2 * HD, TOK), bf16),
            pltpu.VMEM((PLANES, 2 * HD, TOK), bf16),
            pltpu.VMEM((PLANES, 2 * HD, TOK), bf16),
            pltpu.VMEM((2, 2 * HD, TOK), bf16),
        ]
        + [dma((4,))] * 2
        + [dma((PLANES,))] * 6
        + [dma((PLANES, 2))] * 2
        + [dma((PLANES,))] * 6
        + [dma] * 2,
        compiler_params=pltpu.CompilerParams(
            collective_id=0, has_side_effects=True, vmem_limit_bytes=62 << 20
        ),
    )(queries, out_grad, keys, values)
    return pl.pallas_call(
        deliver,
        out_shape=shapes,
        in_specs=[pl.BlockSpec(memory_space=pltpu.VMEM)] * 4,
        out_specs=[pl.BlockSpec(memory_space=pltpu.HBM)] * 4,
        scratch_shapes=[dma((4,))],
        compiler_params=pltpu.CompilerParams(vmem_limit_bytes=62 << 20),
    )(*results)


def solution(mesh):
    spec = P("ctx", "head")
    return jax.shard_map(local, mesh=mesh, in_specs=(spec,) * 4, out_specs=(spec,) * 4, check_vma=False)
```
